512 devices in a mesh: ep: 16 (over y_hi, x, core), blk: 32 (over z, y_lo).
Axes of the slice: x: 4, y: 8 (y_hi: 2, y_lo: 4; y = y_hi * 4 + y_lo), z: 8, core: 2. Of those that a mesh axis runs over, the one named last changes fastest.
Arguments:
- vertex: float32 [524288, 128], P(('ep', 'blk')), parts along dimension 0, may hold values from -2.4 to 2.4
- context: float32 [524288, 128], P(('ep', 'blk')), parts along dimension 0, may hold values from -2.4 to 2.4
- tile_ids: int32 [512, 8, 2], P(('ep', 'blk')), parts along dimension 0, may hold values from 0 to 63, as said below
- live_tiles: int32 [512, 8], P(('ep', 'blk')), parts along dimension 0, may hold values from 1 to 2, as said below
- pos_counts: int32 [512, 8, 2, 128, 128], P(('ep', 'blk')), parts along dimension 0, may hold values from 0 to 3, as said below
- neg_counts: int32 [512, 8, 2, 128, 128], P(('ep', 'blk')), parts along dimension 0, may hold values from 0 to 5, as said below
Outputs:
- new_vertex: float32 [524288, 128], P(('ep', 'blk')), parts along dimension 0
- new_context: float32 [524288, 128], P(('ep', 'blk')), parts along dimension 0
The draws below stay inside these ranges and needn't reach their ends.
There are 16 independent parts, one for each index of `ep`. The reference program is written for one: setup_inputs(seed, part) draws one part's arguments, and reference() takes and returns one part's arrays. A program takes and returns all parts, laid end to end along the dimension named above; each array names one. Nothing has to cross between parts.
Inputs may be any that keep to these rules, and one draw needn't show every extreme that they name: `tile_ids`: for each slice and offset the 2 entries are distinct tile pairs of 0 to 63. `live_tiles`: at every offset some slice has all 2 slots live. `pos_counts`: slots at or above live_tiles hold zeros. `neg_counts`: slots at or above live_tiles hold zeros.
All inputs are finite; a program needn't handle non-finite values.
Results may differ from the reference program's by a relative error of at most 0.0003.
Values sent between devices are 32-bit elements; how exact they have to be, the bound alone decides.
No kernel may reach another device: no remote copies, remote signals or barrier semaphores. Data moves between devices by JAX's collectives and lax.ppermute only.
A program may use at most 64 MiB of HBM per device.

```python
import jax
import jax.numpy as jnp
from jax import lax

DIM = 128
TILE = 128
SLOTS = 2
ROWS_DEV = 1024
PAIRS = 64
SUB = 4
STEPS = 8
NODES = 32768
N_BLK = 32


def live_counts(key):
    first = jax.random.fold_in(key, 101)
    second = jax.random.fold_in(key, 102)
    base = jax.random.randint(first, (N_BLK, STEPS), 1, SLOTS + 1)
    busy = jax.random.randint(second, (STEPS,), 0, N_BLK)
    rows = jnp.arange(N_BLK, dtype=jnp.int32)[:, None]
    return jnp.where(rows == busy[None, :], SLOTS, base).astype(jnp.int32)


def count_draw(key, salt, top):
    live = live_counts(key)
    key = jax.random.fold_in(key, salt)
    values = jax.random.randint(key, (N_BLK, STEPS, SLOTS, TILE, TILE), 0, top)
    mask = jnp.arange(SLOTS, dtype=jnp.int32)[None, None, :] < live[:, :, None]
    return jnp.where(mask[:, :, :, None, None], values, 0).astype(jnp.int32)


def draw_live_tiles(key, part):
    return live_counts(key)


def draw_pos_counts(key, part):
    return count_draw(key, 7, 4)


def draw_neg_counts(key, part):
    return count_draw(key, 9, 6)


def draw_tile_ids(key, part):
    key = jax.random.fold_in(key, 3)
    scores = jax.random.randint(key, (N_BLK, STEPS, PAIRS), 0, 1 << 20) * PAIRS
    scores = scores + jnp.arange(PAIRS, dtype=jnp.int32)[None, None, :]
    order = jnp.argsort(scores, axis=-1, stable=True).astype(jnp.int32)
    chosen = order[:, :, :SLOTS]
    fixed_list = jnp.where(jnp.arange(SLOTS, dtype=jnp.int32) == 0, PAIRS - 1, jnp.arange(SLOTS, dtype=jnp.int32) - 1)
    fixed_list = jnp.where(jnp.arange(SLOTS, dtype=jnp.int32) == 0, PAIRS - 1, fixed_list).astype(jnp.int32)
    first_row = (jnp.arange(N_BLK, dtype=jnp.int32)[:, None] == 0) & (jnp.arange(STEPS, dtype=jnp.int32)[None, :] == 0)
    return jnp.where(first_row[:, :, None], fixed_list[None, None, :], chosen).astype(jnp.int32)


def level_of(key, dims, cuts, low, largest):
    factor_of, own = 1.0, jax.random.fold_in(key, 6)
    for dim, parts in cuts:
        draws = jnp.exp(jax.random.uniform(jax.random.fold_in(own, dim), (parts,), jnp.float32, low / len(cuts), largest / len(cuts)))
        factor_of = factor_of * jnp.repeat(draws, dims[dim] // parts).reshape([-1 if axis == dim else 1 for axis in range(len(dims))])
    return factor_of


def normal_values(stream_key, shape, deviation, reach, cuts=(), kind=jnp.bfloat16):
    result = deviation * jax.random.normal(stream_key, shape, jnp.float32)
    if cuts:
        result = result * level_of(stream_key, shape, cuts, -0.22, 0.18)
    return jnp.clip(result, -reach, reach).astype(kind)


def setup_inputs(seed: int = 0, part: int = 0) -> dict:
    streams_of = jax.random.split(jax.random.key(seed), 7)
    part_splits = jax.random.split(jax.random.fold_in(streams_of[6], part), 7)
    vertex = normal_values(part_splits[0], (NODES, DIM), 0.3, 2.4, ((0, 32),), jnp.float32)
    context = normal_values(part_splits[1], (NODES, DIM), 0.3, 2.4, ((0, 32),), jnp.float32)
    tile_ids = draw_tile_ids(jax.random.fold_in(jax.random.fold_in(streams_of[6], part), 71), part)
    live_tiles = draw_live_tiles(jax.random.fold_in(jax.random.fold_in(streams_of[6], part), 71), part)
    pos_counts = draw_pos_counts(jax.random.fold_in(jax.random.fold_in(streams_of[6], part), 71), part)
    neg_counts = draw_neg_counts(jax.random.fold_in(jax.random.fold_in(streams_of[6], part), 71), part)
    return {"vertex": vertex, "context": context, "tile_ids": tile_ids, "live_tiles": live_tiles, "pos_counts": pos_counts, "neg_counts": neg_counts}


RATES = (0.02, 0.01)


def device_terms(vert, ctx, ids, live, pos, neg):
    tile = pos.shape[-1]
    width = vert.shape[1]
    row_tiles = vert.shape[0] // tile
    slots = ids.shape[0]
    vert_tiles = vert.reshape(row_tiles, tile, width)
    ctx_tiles = ctx.reshape(row_tiles, tile, width)
    which = jnp.arange(row_tiles, dtype=jnp.int32)
    rows_pick = (ids[:, None] // row_tiles == which[None, :]).astype(jnp.float32)
    cols_pick = (ids[:, None] % row_tiles == which[None, :]).astype(jnp.float32)
    high = lax.Precision.HIGHEST
    left = jnp.einsum("sr,rad->sad", rows_pick, vert_tiles, precision=high)
    right = jnp.einsum("sr,rad->sad", cols_pick, ctx_tiles, precision=high)
    score = jnp.einsum("sad,sbd->sab", left, right, precision=high)
    sig = jax.nn.sigmoid(score)
    mask = (jnp.arange(slots, dtype=jnp.int32) < live).astype(jnp.float32)
    grad = neg.astype(jnp.float32) * sig - pos.astype(jnp.float32) * (1.0 - sig)
    grad = grad * mask[:, None, None]
    grad_left = jnp.einsum("sab,sbd->sad", grad, right, precision=high)
    grad_right = jnp.einsum("sab,sad->sbd", grad, left, precision=high)
    vert_grad = jnp.einsum("sr,sad->rad", rows_pick, grad_left, precision=high)
    ctx_grad = jnp.einsum("sr,sad->rad", cols_pick, grad_right, precision=high)
    return vert_grad.reshape(vert.shape), ctx_grad.reshape(ctx.shape)


def reference(vertex, context, tile_ids, live_tiles, pos_counts, neg_counts):
    verts = vertex.reshape(N_BLK, ROWS_DEV, DIM)
    ctxs = context.reshape(N_BLK, ROWS_DEV, DIM)
    for epoch in range(2):
        vert_acc = jnp.zeros_like(verts)
        ctx_acc = jnp.zeros_like(ctxs)
        for inner in range(SUB):
            offset = epoch * SUB + inner
            moved = jnp.roll(ctxs, offset, axis=0)
            vert_grad, ctx_grad = jax.vmap(device_terms)(verts, moved, tile_ids[:, offset], live_tiles[:, offset], pos_counts[:, offset], neg_counts[:, offset])
            vert_acc = vert_acc + vert_grad
            ctx_acc = ctx_acc + jnp.roll(ctx_grad, -offset, axis=0)
        verts = verts - RATES[epoch] * vert_acc
        ctxs = ctxs - RATES[epoch] * ctx_acc
    return verts.reshape(NODES, DIM), ctxs.reshape(NODES, DIM)
```

```python
import jax
import jax.numpy as jnp
from jax import lax
from jax.experimental import pallas as pl
from jax.experimental.pallas import tpu as pltpu
from jax.sharding import PartitionSpec as P

RATES = (0.02, 0.01)
TILE = 128
SLOTS = 2
SUB = 4
VMEM_BYTES = 32 * 1024 * 1024

IN_VMEM = pl.BlockSpec(memory_space=pltpu.VMEM)
IN_SMEM = pl.BlockSpec(memory_space=pltpu.SMEM)
PARAMS = pltpu.CompilerParams(vmem_limit_bytes=VMEM_BYTES)
PAIR = jax.ShapeDtypeStruct((SLOTS, TILE, TILE), jnp.float32)


def tile_rows(index):
    return pl.ds(pl.multiple_of(index * TILE, TILE), TILE)


def from_peer(block, distance):
    size = lax.axis_size("blk")
    return lax.ppermute(block, "blk", [((i + distance) % size, i) for i in range(size)])


def product(left, right, dims):
    return lax.dot_general(
        left,
        right,
        (dims, ((), ())),
        precision=lax.Precision.HIGHEST,
        preferred_element_type=jnp.float32,
    )


def select_columns(context, ids, offset, row_tiles):
    def kernel(ids_ref, context_ref, out_ref):
        for s in range(SLOTS):
            out_ref[s] = context_ref[tile_rows(ids_ref[0, offset, s] % row_tiles), :]

    return pl.pallas_call(
        kernel,
        out_shape=PAIR,
        in_specs=[IN_SMEM, IN_VMEM],
        out_specs=IN_VMEM,
        compiler_params=PARAMS,
        name=f"select_{offset}",
    )(ids, context)


def pair_terms(vert, cols, ids, live, pos, neg, offset, row_tiles):
    def kernel(ids_ref, live_ref, vert_ref, cols_ref, pos_ref, neg_ref, gv_ref, gc_ref):
        for s in range(SLOTS):
            left = vert_ref[tile_rows(ids_ref[0, offset, s] // row_tiles), :]
            right = cols_ref[s]
            score = product(left, right, ((1,), (1,)))
            sig = jax.nn.sigmoid(score)
            pos_f = pos_ref[0, offset, s].astype(jnp.float32)
            neg_f = neg_ref[0, offset, s].astype(jnp.float32)
            grad = neg_f * sig - pos_f * (1.0 - sig)
            grad = jnp.where(s < live_ref[0, offset], grad, 0.0)
            gv_ref[s] = product(grad, right, ((1,), (0,)))
            gc_ref[s] = product(grad, left, ((0,), (0,)))

    return pl.pallas_call(
        kernel,
        out_shape=(PAIR, PAIR),
        in_specs=[IN_SMEM, IN_SMEM] + [IN_VMEM] * 4,
        out_specs=(IN_VMEM, IN_VMEM),
        compiler_params=PARAMS,
        name=f"terms_{offset}",
    )(ids, live, vert, cols, pos, neg)


def apply_vertex(vert, ids, grads, epoch, row_tiles):
    def kernel(ids_ref, vert_ref, *refs):
        *grad_refs, out_ref = refs
        out_ref[...] = vert_ref[...]
        for inner, grad_ref in enumerate(grad_refs):
            for s in range(SLOTS):
                rows = tile_rows(ids_ref[0, epoch * SUB + inner, s] // row_tiles)
                out_ref[rows, :] -= RATES[epoch] * grad_ref[s]

    return pl.pallas_call(
        kernel,
        out_shape=jax.ShapeDtypeStruct(vert.shape, vert.dtype),
        in_specs=[IN_SMEM, IN_VMEM] + [IN_VMEM] * len(grads),
        out_specs=IN_VMEM,
        compiler_params=PARAMS,
        name=f"vertex_{epoch}",
    )(ids, vert, *grads)


def apply_context(ctx, ids, grads, epoch, row_tiles, sends):
    n = len(grads)

    def kernel(*refs):
        id_refs, send_refs = refs[:n], refs[n : n + len(sends)]
        ctx_ref, *grad_refs = refs[n + len(sends) : 2 * n + len(sends) + 1]
        out_ref, *tile_refs = refs[2 * n + len(sends) + 1 :]
        out_ref[...] = ctx_ref[...]
        for inner in range(n):
            for s in range(SLOTS):
                rows = tile_rows(id_refs[inner][0, epoch * SUB + inner, s] % row_tiles)
                out_ref[rows, :] -= RATES[epoch] * grad_refs[inner][s]
        for (_, offset), send_ref, tile_ref in zip(sends, send_refs, tile_refs):
            for s in range(SLOTS):
                tile_ref[s] = out_ref[tile_rows(send_ref[0, offset, s] % row_tiles), :]

    return pl.pallas_call(
        kernel,
        out_shape=(jax.ShapeDtypeStruct(ctx.shape, ctx.dtype),) + (PAIR,) * len(sends),
        in_specs=[IN_SMEM] * (n + len(sends)) + [IN_VMEM] * (n + 1),
        out_specs=(IN_VMEM,) * (1 + len(sends)),
        compiler_params=PARAMS,
        name=f"context_{epoch}",
    )(*ids, *[peer for peer, _ in sends], ctx, *grads)


def per_device(vertex, context, tile_ids, live_tiles, pos_counts, neg_counts):
    row_tiles = vertex.shape[0] // TILE
    peer_ids = {0: tile_ids}
    for k in range(1, SUB):
        peer_ids[k] = from_peer(tile_ids, k)
    near = jnp.concatenate([peer_ids[k] for k in range(SUB)], axis=0)
    far = from_peer(near, SUB)
    for k in range(SUB):
        peer_ids[SUB + k] = far[k : k + 1]

    vert, ctx = vertex, context
    sends = {k: select_columns(ctx, peer_ids[k], k, row_tiles) for k in range(SUB)}
    for epoch in range(2):
        vert_grads, ctx_grads = [], []
        offsets = range(epoch * SUB, (epoch + 1) * SUB)
        for k in offsets:
            cols = from_peer(sends[k], -k) if k else sends[k]
            gv, gc = pair_terms(vert, cols, tile_ids, live_tiles, pos_counts, neg_counts, k, row_tiles)
            vert_grads.append(gv)
            ctx_grads.append(from_peer(gc, k) if k else gc)
        vert = apply_vertex(vert, tile_ids, vert_grads, epoch, row_tiles)
        following = range(SUB, 2 * SUB) if epoch == 0 else ()
        ctx, *tiles = apply_context(
            ctx,
            [peer_ids[k] for k in offsets],
            ctx_grads,
            epoch,
            row_tiles,
            [(peer_ids[k], k) for k in following],
        )
        sends = dict(zip(following, tiles))
    return vert, ctx


def solution(mesh):
    placed = (
        P(("ep", "blk"), None),
        P(("ep", "blk"), None),
        P(("ep", "blk"), None, None),
        P(("ep", "blk"), None),
        P(("ep", "blk"), None, None, None, None),
        P(("ep", "blk"), None, None, None, None),
    )
    return jax.shard_map(
        per_device,
        mesh=mesh,
        in_specs=placed,
        out_specs=(P(("ep", "blk"), None), P(("ep", "blk"), None)),
        check_vma=False,
    )
```

```python
import jax
import jax.numpy as jnp
from jax import lax
from jax.experimental import pallas as pl
from jax.experimental.pallas import tpu as pltpu
from jax.sharding import PartitionSpec as P

RATES = (0.02, 0.01)
TILE = 128
SLOTS = 2
SUB = 4
STEPS = 2 * SUB
CLASSES = (3, 2, 1, 0)
OTHERS = (3, 2, 1)
PAIR_ROWS = SLOTS * TILE
META = 32
LIVE_AT = SLOTS * STEPS
ODD_AT = LIVE_AT + STEPS
NOTE_ROWS = 8
VMEM_BYTES = 8 * 1024 * 1024

IN_VMEM = pl.BlockSpec(memory_space=pltpu.VMEM)
IN_SMEM = pl.BlockSpec(memory_space=pltpu.SMEM)
IN_HBM = pl.BlockSpec(memory_space=pltpu.HBM)
PARAMS = pltpu.CompilerParams(vmem_limit_bytes=VMEM_BYTES)
PAIR = jax.ShapeDtypeStruct((PAIR_ROWS, TILE), jnp.float32)
NOTED = jax.ShapeDtypeStruct((PAIR_ROWS + NOTE_ROWS, TILE), jnp.float32)
COUNTS = jax.ShapeDtypeStruct((2 * PAIR_ROWS + NOTE_ROWS, TILE), jnp.float32)


def ahead(place, cls):
    return ((place ^ ((SUB - cls) % SUB)) - place) & (SUB - 1)


def to_users(block, cls, extra=0):
    size = lax.axis_size("blk")
    return lax.ppermute(block, "blk", [(j, (j + ahead(j % SUB, cls) + extra) % size) for j in range(size)])


def to_owners(block, cls, extra=0):
    size = lax.axis_size("blk")
    return lax.ppermute(block, "blk", [((j + ahead(j % SUB, cls) + extra) % size, j) for j in range(size)])


def user_offset(cls, epoch, odd):
    return SUB * epoch + (0, 1 + 2 * odd, 2, 3 - 2 * odd)[cls]


def owner_offset(cls, epoch, odd):
    return SUB * epoch + (0, 3 - 2 * odd, 2, 1 + 2 * odd)[cls]


def tile_rows(index):
    return pl.ds(pl.multiple_of(index * TILE, TILE), TILE)


def slot_rows(slot, part=0):
    return pl.ds(part * PAIR_ROWS + slot * TILE, TILE)


def split(x):
    high = x.astype(jnp.bfloat16)
    return high, (x - high.astype(jnp.float32)).astype(jnp.bfloat16)


def product(left, right, dims):
    def dot(a, b):
        return lax.dot_general(a, b, (dims, ((), ())), preferred_element_type=jnp.float32)

    return dot(left[0], right[0]) + (dot(left[0], right[1]) + dot(left[1], right[0]))


def slot_terms(left, right, pos, neg):
    left, right = split(left), split(right)
    sig = jax.nn.sigmoid(product(left, right, ((1,), (1,))))
    grad = split(neg * sig - pos * (1.0 - sig))
    return product(grad, right, ((1,), (0,))), product(grad, left, ((0,), (0,)))


def call(kernel, name, out_shape, in_specs, args, cost, scratch=()):
    several = isinstance(out_shape, tuple)
    return pl.pallas_call(
        kernel,
        out_shape=out_shape,
        in_specs=in_specs,
        out_specs=(IN_VMEM,) * len(out_shape) if several else IN_VMEM,
        scratch_shapes=scratch,
        compiler_params=PARAMS,
        cost_estimate=pl.CostEstimate(flops=int(cost * 1e9), bytes_accessed=0, transcendentals=0),
        name=name,
    )(*args)


def in_hbm(x):
    return pltpu.with_memory_space_constraint(x, pltpu.HBM)


def note_rows(values):
    row = lax.broadcasted_iota(jnp.int32, (NOTE_ROWS, TILE), 0)
    note = jnp.zeros((NOTE_ROWS, TILE), jnp.int32)
    for n, value in enumerate(values):
        note = jnp.where(row == n, value, note)
    return note.astype(jnp.float32)


def stage_pairs(meta, vert, ctx, pos, neg, row_tiles):
    def kernel(meta_ref, vert_ref, ctx_ref, pos_ref, neg_ref, *refs):
        own_ref, vert_refs = refs[0], refs[1 : 1 + SUB]
        count_refs = refs[1 + SUB : -2]
        staged, sems = refs[-2:]
        odd = meta_ref[ODD_AT]
        copies = []
        for n, ref in enumerate((pos_ref, neg_ref)):
            copies.append(pltpu.make_async_copy(ref.at[0], staged.at[n], sems.at[n]))
        for s in range(SLOTS):
            rows = tile_rows(meta_ref[s * STEPS] % row_tiles)
            copies.append(pltpu.make_async_copy(ctx_ref.at[rows], own_ref.at[slot_rows(s)], sems.at[len(copies)]))
        for cls, out_ref in zip(CLASSES, vert_refs):
            for s in range(SLOTS):
                rows = tile_rows(meta_ref[s * STEPS + user_offset(cls, 0, odd)] // row_tiles)
                copies.append(pltpu.make_async_copy(vert_ref.at[rows], out_ref.at[slot_rows(s)], sems.at[len(copies)]))
        for copy in copies:
            copy.start()
        for copy in copies:
            copy.wait()
        for m, out_ref in enumerate(count_refs):
            k = user_offset(CLASSES[m % SUB], m // SUB, odd)
            for n in range(2):
                for s in range(SLOTS):
                    live = s < meta_ref[LIVE_AT + k]
                    out_ref[slot_rows(s, n), :] = jnp.where(live, staged[n, k, s].astype(jnp.float32), 0.0)
            out_ref[2 * PAIR_ROWS :, :] = note_rows([meta_ref[s * STEPS + k] % row_tiles for s in range(SLOTS)])

    n_copies = 2 + SLOTS * (1 + SUB)
    own, *rest = call(
        kernel,
        "stage",
        (PAIR,) * (1 + SUB) + (COUNTS,) * (2 * SUB),
        [IN_SMEM] + [IN_HBM] * 4,
        [meta, in_hbm(vert), in_hbm(ctx), in_hbm(pos), in_hbm(neg)],
        2,
        [pltpu.VMEM((2, STEPS, SLOTS, TILE, TILE), jnp.int32), pltpu.SemaphoreType.DMA((n_copies,))],
    )
    keys = [(cls, epoch) for epoch in range(2) for cls in CLASSES]
    return own, dict(zip(CLASSES, rest)), dict(zip(keys, rest[SUB:]))


def select_columns(meta, ctx, cls, row_tiles):
    def kernel(meta_ref, ctx_ref, out_ref):
        k = user_offset(cls, 0, meta_ref[ODD_AT])
        for s in range(SLOTS):
            out_ref[slot_rows(s), :] = ctx_ref[tile_rows(meta_ref[s * STEPS + k] % row_tiles), :]

    return call(kernel, f"select_{cls}", PAIR, [IN_SMEM, IN_VMEM], [meta, ctx], 1)


def pair_terms(rows, cols, counts, noted, name):
    def kernel(rows_ref, cols_ref, counts_ref, gv_ref, gc_ref):
        for s in range(SLOTS):
            gv_ref[slot_rows(s), :], gc_ref[slot_rows(s), :] = slot_terms(
                rows_ref[slot_rows(s), :],
                cols_ref[slot_rows(s), :],
                counts_ref[slot_rows(s), :],
                counts_ref[slot_rows(s, 1), :],
            )
        if noted:
            gc_ref[PAIR_ROWS:, :] = counts_ref[2 * PAIR_ROWS :, :]

    return call(kernel, name, (PAIR, NOTED if noted else PAIR), [IN_VMEM] * 3, [rows, cols, counts], 4)


def apply_vertex(meta, vert, grads, epoch, row_tiles):
    def kernel(meta_ref, vert_ref, *refs):
        grad_refs, out_ref, next_refs = refs[:SUB], refs[SUB], refs[SUB + 1 :]
        odd = meta_ref[ODD_AT]
        out_ref[...] = vert_ref[...]
        for cls, grad_ref in zip(CLASSES, grad_refs):
            for s in range(SLOTS):
                rows = tile_rows(meta_ref[s * STEPS + user_offset(cls, epoch, odd)] // row_tiles)
                out_ref[rows, :] -= RATES[epoch] * grad_ref[slot_rows(s), :]
        for cls, next_ref in zip(CLASSES, next_refs):
            for s in range(SLOTS):
                rows = tile_rows(meta_ref[s * STEPS + user_offset(cls, 1, odd)] // row_tiles)
                next_ref[slot_rows(s), :] = out_ref[rows, :]

    shapes = (jax.ShapeDtypeStruct(vert.shape, vert.dtype),) + (PAIR,) * (SUB if epoch == 0 else 0)
    args = [meta, vert] + [grads[cls] for cls in CLASSES]
    return call(kernel, f"vertex_{epoch}", shapes, [IN_SMEM] + [IN_VMEM] * (1 + SUB), args, 1)


def first_context(meta, ctx, grad, row_tiles):
    def kernel(meta_ref, ctx_ref, grad_ref, out_ref):
        out_ref[...] = ctx_ref[...]
        for s in range(SLOTS):
            out_ref[tile_rows(meta_ref[s * STEPS] % row_tiles), :] -= RATES[0] * grad_ref[slot_rows(s), :]

    shape = jax.ShapeDtypeStruct(ctx.shape, ctx.dtype)
    return call(kernel, "first_context", shape, [IN_SMEM] + [IN_VMEM] * 2, [meta, ctx, grad], 1)


def gather_context(near, ctx, grads, row_tiles):
    def kernel(near_ref, ctx_ref, *refs):
        grad_refs, out_ref, send_refs = refs[: SUB - 1], refs[SUB - 1], refs[SUB:]
        odd = near_ref[0, ODD_AT]
        tiles = []
        for grad_ref in grad_refs:
            for s in range(SLOTS):
                tiles.append(jnp.max(grad_ref[PAIR_ROWS + s : PAIR_ROWS + s + 1, :]).astype(jnp.int32))
        out_ref[...] = ctx_ref[...]
        for n, grad_ref in enumerate(grad_refs):
            for s in range(SLOTS):
                out_ref[tile_rows(tiles[n * SLOTS + s]), :] -= RATES[0] * grad_ref[slot_rows(s), :]
        for cls, send_ref in zip(CLASSES, send_refs):
            for s in range(SLOTS):
                tile = near_ref[cls, s * STEPS + owner_offset(cls, 1, odd)] % row_tiles
                send_ref[slot_rows(s), :] = out_ref[tile_rows(tile), :]

    shapes = (jax.ShapeDtypeStruct(ctx.shape, ctx.dtype),) + (PAIR,) * SUB
    return call(kernel, "gather_context", shapes, [IN_SMEM] + [IN_VMEM] * SUB, [near, ctx, *grads], 1)


def returned_context(near, ctx, grad, row_tiles):
    rows = ctx.shape[0]

    def kernel(near_ref, ctx_ref, grad_ref, out_ref):
        odd = near_ref[0, ODD_AT]
        out_ref[:rows, :] = ctx_ref[...]
        for s in range(SLOTS):
            tile = tile_rows(near_ref[0, s * STEPS + SUB] % row_tiles)
            out_ref[tile, :] -= RATES[1] * grad_ref[slot_rows(s), :]
        notes = []
        for cls in OTHERS:
            for s in range(SLOTS):
                notes.append(near_ref[cls, s * STEPS + owner_offset(cls, 1, odd)] % row_tiles)
        out_ref[rows:, :] = note_rows(notes)

    shape = jax.ShapeDtypeStruct((rows + NOTE_ROWS, TILE), ctx.dtype)
    return call(kernel, "returned_context", shape, [IN_SMEM] + [IN_VMEM] * 2, [near, ctx, grad], 1)


def last_context(notes, ctx, grads):
    rows = ctx.shape[0] - NOTE_ROWS

    def kernel(notes_ref, ctx_ref, *refs):
        *grad_refs, out_ref = refs
        out_ref[...] = ctx_ref[:rows, :]
        for n, grad_ref in enumerate(grad_refs):
            for s in range(SLOTS):
                out_ref[tile_rows(notes_ref[n * SLOTS + s]), :] -= RATES[1] * grad_ref[slot_rows(s), :]

    shape = jax.ShapeDtypeStruct((rows, TILE), ctx.dtype)
    return call(kernel, "last_context", shape, [IN_SMEM] + [IN_VMEM] * SUB, [notes, ctx, *grads], 1)


def per_device(vertex, context, tile_ids, live_tiles, pos_counts, neg_counts):
    row_tiles = vertex.shape[0] // TILE
    odd = (lax.axis_index("blk") & 1)[None]
    pad = jnp.zeros((META - ODD_AT - 1,), jnp.int32)
    meta = jnp.concatenate([jnp.swapaxes(tile_ids, 1, 2).reshape(-1), live_tiles.reshape(-1), odd, pad])

    ids = {0: meta}
    for cls in OTHERS:
        ids[cls] = to_owners(meta, cls)
    ids[3], ids[2], ids[1] = lax.optimization_barrier((ids[3], ids[2], ids[1]))
    own, rows, counts = stage_pairs(meta, vertex, context, pos_counts, neg_counts, row_tiles)
    cols = {cls: to_users(select_columns(ids[cls], context, cls, row_tiles), cls) for cls in OTHERS}
    gv, gc = {}, {}
    gv[0], gc[0] = pair_terms(rows[0], own, counts[0, 0], False, "terms_0_0")
    handed = to_users(first_context(meta, context, gc[0], row_tiles), 0, SUB)
    for cls in OTHERS:
        gv[cls], gc[cls] = pair_terms(rows[cls], cols[cls], counts[cls, 0], True, f"terms_0_{cls}")
        gc[cls] = to_users(gc[cls], cls)
    near = jnp.stack([ids[cls] for cls in range(SUB)])
    vert, *rows = apply_vertex(meta, vertex, gv, 0, row_tiles)
    ctx, *cols = gather_context(near, handed, [gc[cls] for cls in OTHERS], row_tiles)

    rows, cols = dict(zip(CLASSES, rows)), dict(zip(CLASSES, cols))
    cols.update({cls: to_users(cols[cls], cls) for cls in OTHERS})
    gv[0], gc[0] = pair_terms(rows[0], cols[0], counts[0, 1], False, "terms_1_0")
    back = to_owners(returned_context(near, ctx, gc[0], row_tiles), 0, SUB)
    notes = back[-NOTE_ROWS:, 0].astype(jnp.int32)
    for cls in OTHERS:
        gv[cls], grad = pair_terms(rows[cls], cols[cls], counts[cls, 1], False, f"terms_1_{cls}")
        gc[cls] = to_owners(grad, cls, SUB)
    (vert,) = apply_vertex(meta, vert, gv, 1, row_tiles)
    ctx = last_context(notes, back, [gc[cls] for cls in OTHERS])
    return vert, ctx


def solution(mesh):
    placed = (
        P(("ep", "blk"), None),
        P(("ep", "blk"), None),
        P(("ep", "blk"), None, None),
        P(("ep", "blk"), None),
        P(("ep", "blk"), None, None, None, None),
        P(("ep", "blk"), None, None, None, None),
    )
    return jax.shard_map(
        per_device,
        mesh=mesh,
        in_specs=placed,
        out_specs=(P(("ep", "blk"), None), P(("ep", "blk"), None)),
        check_vma=False,
    )
```

```python
import jax
import jax.numpy as jnp
from jax import lax
from jax.experimental import pallas as pl
from jax.experimental.pallas import tpu as pltpu
from jax.sharding import PartitionSpec as P

RATES = (0.02, 0.01)
TILE = 128
SLOTS = 2
SUB = 4
STEPS = 2 * SUB
CLASSES = (3, 2, 1, 0)
OTHERS = (3, 2, 1)
PAIR_ROWS = SLOTS * TILE
META = 32
ODD_AT = SLOTS * STEPS
NOTE_ROWS = 8
VMEM_BYTES = 8 * 1024 * 1024

IN_VMEM = pl.BlockSpec(memory_space=pltpu.VMEM)
IN_SMEM = pl.BlockSpec(memory_space=pltpu.SMEM)
IN_HBM = pl.BlockSpec(memory_space=pltpu.HBM)
PARAMS = pltpu.CompilerParams(vmem_limit_bytes=VMEM_BYTES)
PAIR = jax.ShapeDtypeStruct((PAIR_ROWS, TILE), jnp.float32)
NOTED = jax.ShapeDtypeStruct((PAIR_ROWS + NOTE_ROWS, TILE), jnp.float32)
COUNTS = jax.ShapeDtypeStruct((2 * PAIR_ROWS + NOTE_ROWS, TILE), jnp.float32)


def ahead(place, cls):
    return ((place ^ ((SUB - cls) % SUB)) - place) & (SUB - 1)


def to_users(block, cls, extra=0):
    size = lax.axis_size("blk")
    return lax.ppermute(block, "blk", [(j, (j + ahead(j % SUB, cls) + extra) % size) for j in range(size)])


def to_owners(block, cls, extra=0):
    size = lax.axis_size("blk")
    return lax.ppermute(block, "blk", [((j + ahead(j % SUB, cls) + extra) % size, j) for j in range(size)])


def user_offset(cls, epoch, odd):
    return SUB * epoch + (0, 1 + 2 * odd, 2, 3 - 2 * odd)[cls]


def owner_offset(cls, epoch, odd):
    return SUB * epoch + (0, 3 - 2 * odd, 2, 1 + 2 * odd)[cls]


def tile_rows(index):
    return pl.ds(pl.multiple_of(index * TILE, TILE), TILE)


def slot_rows(slot, part=0):
    return pl.ds(part * PAIR_ROWS + slot * TILE, TILE)


def split(x):
    high = x.astype(jnp.bfloat16)
    return high, (x - high.astype(jnp.float32)).astype(jnp.bfloat16)


def product(left, right, dims):
    def dot(a, b):
        return lax.dot_general(a, b, (dims, ((), ())), preferred_element_type=jnp.float32)

    return dot(left[0], right[0]) + (dot(left[0], right[1]) + dot(left[1], right[0]))


def slot_terms(left, right, pos, neg):
    left, right = split(left), split(right)
    sig = jax.nn.sigmoid(product(left, right, ((1,), (1,))))
    grad = split(neg * sig - pos * (1.0 - sig))
    return product(grad, right, ((1,), (0,))), product(grad, left, ((0,), (0,)))


def call(kernel, name, out_shape, in_specs, args, cost, scratch=()):
    several = isinstance(out_shape, tuple)
    return pl.pallas_call(
        kernel,
        out_shape=out_shape,
        in_specs=in_specs,
        out_specs=(IN_VMEM,) * len(out_shape) if several else IN_VMEM,
        scratch_shapes=scratch,
        compiler_params=PARAMS,
        cost_estimate=pl.CostEstimate(flops=int(cost * 1e9), bytes_accessed=0, transcendentals=0),
        name=name,
    )(*args)


def in_hbm(x):
    return pltpu.with_memory_space_constraint(x, pltpu.HBM)


def note_rows(values):
    row = lax.broadcasted_iota(jnp.int32, (NOTE_ROWS, TILE), 0)
    note = jnp.zeros((NOTE_ROWS, TILE), jnp.int32)
    for n, value in enumerate(values):
        note = jnp.where(row == n, value, note)
    return note.astype(jnp.float32)


def stage_pairs(meta, live, vert, ctx, pos, neg, row_tiles):
    def kernel(meta_ref, live_ref, vert_ref, ctx_ref, pos_ref, neg_ref, *refs):
        own_ref, vert_refs = refs[0], refs[1 : 1 + SUB]
        count_refs = refs[1 + SUB : -2]
        staged, sems = refs[-2:]
        odd = meta_ref[ODD_AT]
        copies = []
        for n, ref in enumerate((pos_ref, neg_ref)):
            copies.append(pltpu.make_async_copy(ref.at[0], staged.at[n], sems.at[n]))
        for s in range(SLOTS):
            rows = tile_rows(meta_ref[s * STEPS] % row_tiles)
            copies.append(pltpu.make_async_copy(ctx_ref.at[rows], own_ref.at[slot_rows(s)], sems.at[len(copies)]))
        for cls, out_ref in zip(CLASSES, vert_refs):
            for s in range(SLOTS):
                rows = tile_rows(meta_ref[s * STEPS + user_offset(cls, 0, odd)] // row_tiles)
                copies.append(pltpu.make_async_copy(vert_ref.at[rows], out_ref.at[slot_rows(s)], sems.at[len(copies)]))
        for copy in copies:
            copy.start()
        for copy in copies:
            copy.wait()
        for m, out_ref in enumerate(count_refs):
            k = user_offset(CLASSES[m % SUB], m // SUB, odd)
            for n in range(2):
                for s in range(SLOTS):
                    live = s < live_ref[0, k]
                    out_ref[slot_rows(s, n), :] = jnp.where(live, staged[n, k, s].astype(jnp.float32), 0.0)
            out_ref[2 * PAIR_ROWS :, :] = note_rows([meta_ref[s * STEPS + k] % row_tiles for s in range(SLOTS)])

    n_copies = 2 + SLOTS * (1 + SUB)
    own, *rest = call(
        kernel,
        "stage",
        (PAIR,) * (1 + SUB) + (COUNTS,) * (2 * SUB),
        [IN_SMEM] * 2 + [IN_HBM] * 4,
        [meta, live, in_hbm(vert), in_hbm(ctx), in_hbm(pos), in_hbm(neg)],
        2,
        [pltpu.VMEM((2, STEPS, SLOTS, TILE, TILE), jnp.int32), pltpu.SemaphoreType.DMA((n_copies,))],
    )
    keys = [(cls, epoch) for epoch in range(2) for cls in CLASSES]
    return own, dict(zip(CLASSES, rest)), dict(zip(keys, rest[SUB:]))


def select_columns(meta, ctx, cls, row_tiles):
    def kernel(meta_ref, ctx_ref, out_ref):
        k = user_offset(cls, 0, meta_ref[ODD_AT])
        for s in range(SLOTS):
            out_ref[slot_rows(s), :] = ctx_ref[tile_rows(meta_ref[s * STEPS + k] % row_tiles), :]

    return call(kernel, f"select_{cls}", PAIR, [IN_SMEM, IN_VMEM], [meta, ctx], 1)


def pair_terms(rows, cols, counts, noted, name):
    def kernel(rows_ref, cols_ref, counts_ref, gv_ref, gc_ref):
        for s in range(SLOTS):
            gv_ref[slot_rows(s), :], gc_ref[slot_rows(s), :] = slot_terms(
                rows_ref[slot_rows(s), :],
                cols_ref[slot_rows(s), :],
                counts_ref[slot_rows(s), :],
                counts_ref[slot_rows(s, 1), :],
            )
        if noted:
            gc_ref[PAIR_ROWS:, :] = counts_ref[2 * PAIR_ROWS :, :]

    return call(kernel, name, (PAIR, NOTED if noted else PAIR), [IN_VMEM] * 3, [rows, cols, counts], 4)


def apply_vertex(meta, vert, grads, epoch, row_tiles):
    def kernel(meta_ref, vert_ref, *refs):
        grad_refs, out_ref, next_refs = refs[:SUB], refs[SUB], refs[SUB + 1 :]
        odd = meta_ref[ODD_AT]
        out_ref[...] = vert_ref[...]
        for cls, grad_ref in zip(CLASSES, grad_refs):
            for s in range(SLOTS):
                rows = tile_rows(meta_ref[s * STEPS + user_offset(cls, epoch, odd)] // row_tiles)
                out_ref[rows, :] -= RATES[epoch] * grad_ref[slot_rows(s), :]
        for cls, next_ref in zip(CLASSES, next_refs):
            for s in range(SLOTS):
                rows = tile_rows(meta_ref[s * STEPS + user_offset(cls, 1, odd)] // row_tiles)
                next_ref[slot_rows(s), :] = out_ref[rows, :]

    shapes = (jax.ShapeDtypeStruct(vert.shape, vert.dtype),) + (PAIR,) * (SUB if epoch == 0 else 0)
    args = [meta, vert] + [grads[cls] for cls in CLASSES]
    return call(kernel, f"vertex_{epoch}", shapes, [IN_SMEM] + [IN_VMEM] * (1 + SUB), args, 1)


def first_context(meta, ctx, grad, row_tiles):
    def kernel(meta_ref, ctx_ref, grad_ref, out_ref):
        out_ref[...] = ctx_ref[...]
        for s in range(SLOTS):
            out_ref[tile_rows(meta_ref[s * STEPS] % row_tiles), :] -= RATES[0] * grad_ref[slot_rows(s), :]

    shape = jax.ShapeDtypeStruct(ctx.shape, ctx.dtype)
    return call(kernel, "first_context", shape, [IN_SMEM] + [IN_VMEM] * 2, [meta, ctx, grad], 1)


def gather_context(near, ctx, grads, row_tiles):
    def kernel(near_ref, ctx_ref, *refs):
        grad_refs, out_ref, send_refs = refs[: SUB - 1], refs[SUB - 1], refs[SUB:]
        odd = near_ref[0, ODD_AT]
        tiles = []
        for grad_ref in grad_refs:
            for s in range(SLOTS):
                tiles.append(jnp.max(grad_ref[PAIR_ROWS + s : PAIR_ROWS + s + 1, :]).astype(jnp.int32))
        out_ref[...] = ctx_ref[...]
        for n, grad_ref in enumerate(grad_refs):
            for s in range(SLOTS):
                out_ref[tile_rows(tiles[n * SLOTS + s]), :] -= RATES[0] * grad_ref[slot_rows(s), :]
        for cls, send_ref in zip(CLASSES, send_refs):
            for s in range(SLOTS):
                tile = near_ref[cls, s * STEPS + owner_offset(cls, 1, odd)] % row_tiles
                send_ref[slot_rows(s), :] = out_ref[tile_rows(tile), :]

    shapes = (jax.ShapeDtypeStruct(ctx.shape, ctx.dtype),) + (PAIR,) * SUB
    return call(kernel, "gather_context", shapes, [IN_SMEM] + [IN_VMEM] * SUB, [near, ctx, *grads], 1)


def returned_context(near, ctx, grad, row_tiles):
    rows = ctx.shape[0]

    def kernel(near_ref, ctx_ref, grad_ref, out_ref):
        odd = near_ref[0, ODD_AT]
        out_ref[:rows, :] = ctx_ref[...]
        for s in range(SLOTS):
            tile = tile_rows(near_ref[0, s * STEPS + SUB] % row_tiles)
            out_ref[tile, :] -= RATES[1] * grad_ref[slot_rows(s), :]
        notes = []
        for cls in OTHERS:
            for s in range(SLOTS):
                notes.append(near_ref[cls, s * STEPS + owner_offset(cls, 1, odd)] % row_tiles)
        out_ref[rows:, :] = note_rows(notes)

    shape = jax.ShapeDtypeStruct((rows + NOTE_ROWS, TILE), ctx.dtype)
    return call(kernel, "returned_context", shape, [IN_SMEM] + [IN_VMEM] * 2, [near, ctx, grad], 1)


def last_context(notes, ctx, grads):
    rows = ctx.shape[0] - NOTE_ROWS

    def kernel(notes_ref, ctx_ref, *refs):
        *grad_refs, out_ref = refs
        out_ref[...] = ctx_ref[:rows, :]
        for n, grad_ref in enumerate(grad_refs):
            for s in range(SLOTS):
                out_ref[tile_rows(notes_ref[n * SLOTS + s]), :] -= RATES[1] * grad_ref[slot_rows(s), :]

    shape = jax.ShapeDtypeStruct((rows, TILE), ctx.dtype)
    return call(kernel, "last_context", shape, [IN_SMEM] + [IN_VMEM] * SUB, [notes, ctx, *grads], 1)


def per_device(vertex, context, tile_ids, live_tiles, pos_counts, neg_counts):
    row_tiles = vertex.shape[0] // TILE
    odd = (lax.axis_index("blk") & 1)[None]
    pad = jnp.zeros((META - ODD_AT - 1,), jnp.int32)
    meta = jnp.concatenate([jnp.swapaxes(tile_ids, 1, 2).reshape(-1), odd, pad])

    ids = {0: meta}
    for cls in OTHERS:
        ids[cls] = to_owners(meta, cls)
    ids[3], ids[2], ids[1] = lax.optimization_barrier((ids[3], ids[2], ids[1]))
    own, rows, counts = stage_pairs(meta, live_tiles, vertex, context, pos_counts, neg_counts, row_tiles)
    cols = {cls: to_users(select_columns(ids[cls], context, cls, row_tiles), cls) for cls in OTHERS}
    gv, gc = {}, {}
    gv[0], gc[0] = pair_terms(rows[0], own, counts[0, 0], False, "terms_0_0")
    handed = to_users(first_context(meta, context, gc[0], row_tiles), 0, SUB)
    for cls in OTHERS:
        gv[cls], gc[cls] = pair_terms(rows[cls], cols[cls], counts[cls, 0], True, f"terms_0_{cls}")
        gc[cls] = to_users(gc[cls], cls)
    near = jnp.stack([ids[cls] for cls in range(SUB)])
    vert, *rows = apply_vertex(meta, vertex, gv, 0, row_tiles)
    ctx, *cols = gather_context(near, handed, [gc[cls] for cls in OTHERS], row_tiles)

    rows, cols = dict(zip(CLASSES, rows)), dict(zip(CLASSES, cols))
    cols.update({cls: to_users(cols[cls], cls) for cls in OTHERS})
    gv[0], gc[0] = pair_terms(rows[0], cols[0], counts[0, 1], False, "terms_1_0")
    back = to_owners(returned_context(near, ctx, gc[0], row_tiles), 0, SUB)
    notes = back[-NOTE_ROWS:, 0].astype(jnp.int32)
    for cls in OTHERS:
        gv[cls], grad = pair_terms(rows[cls], cols[cls], counts[cls, 1], False, f"terms_1_{cls}")
        gc[cls] = to_owners(grad, cls, SUB)
    (vert,) = apply_vertex(meta, vert, gv, 1, row_tiles)
    ctx = last_context(notes, back, [gc[cls] for cls in OTHERS])
    return vert, ctx


def solution(mesh):
    placed = (
        P(("ep", "blk"), None),
        P(("ep", "blk"), None),
        P(("ep", "blk"), None, None),
        P(("ep", "blk"), None),
        P(("ep", "blk"), None, None, None, None),
        P(("ep", "blk"), None, None, None, None),
    )
    return jax.shard_map(
        per_device,
        mesh=mesh,
        in_specs=placed,
        out_specs=(P(("ep", "blk"), None), P(("ep", "blk"), None)),
        check_vma=False,
    )
```

```python
import jax
import jax.numpy as jnp
from jax import lax
from jax.experimental import pallas as pl
from jax.experimental.pallas import tpu as pltpu
from jax.sharding import PartitionSpec as P

RATES = (0.02, 0.01)
TILE = 128
SLOTS = 2
SUB = 4
STEPS = 2 * SUB
CLASSES = (3, 2, 1, 0)
OTHERS = (3, 2, 1)
PAIR_ROWS = SLOTS * TILE
META = 32
ODD_AT = SLOTS * STEPS
NOTE_ROWS = 8
VMEM_BYTES = 8 * 1024 * 1024

IN_VMEM = pl.BlockSpec(memory_space=pltpu.VMEM)
IN_SMEM = pl.BlockSpec(memory_space=pltpu.SMEM)
IN_HBM = pl.BlockSpec(memory_space=pltpu.HBM)
PARAMS = pltpu.CompilerParams(vmem_limit_bytes=VMEM_BYTES)
PAIR = jax.ShapeDtypeStruct((PAIR_ROWS, TILE), jnp.float32)
NOTED = jax.ShapeDtypeStruct((PAIR_ROWS + NOTE_ROWS, TILE), jnp.float32)
COUNTS = jax.ShapeDtypeStruct((2 * PAIR_ROWS + NOTE_ROWS, TILE), jnp.float32)


def ahead(place, cls):
    return ((place ^ ((SUB - cls) % SUB)) - place) & (SUB - 1)


def to_users(block, cls, extra=0):
    size = lax.axis_size("blk")
    return lax.ppermute(block, "blk", [(j, (j + ahead(j % SUB, cls) + extra) % size) for j in range(size)])


def to_owners(block, cls, extra=0):
    size = lax.axis_size("blk")
    return lax.ppermute(block, "blk", [((j + ahead(j % SUB, cls) + extra) % size, j) for j in range(size)])


def user_offset(cls, epoch, odd):
    return SUB * epoch + (0, 1 + 2 * odd, 2, 3 - 2 * odd)[cls]


def owner_offset(cls, epoch, odd):
    return SUB * epoch + (0, 3 - 2 * odd, 2, 1 + 2 * odd)[cls]


def tile_rows(index):
    return pl.ds(pl.multiple_of(index * TILE, TILE), TILE)


def slot_rows(slot, part=0):
    return pl.ds(part * PAIR_ROWS + slot * TILE, TILE)


def split(x):
    high = x.astype(jnp.bfloat16)
    return high, (x - high.astype(jnp.float32)).astype(jnp.bfloat16)


def product(left, right, dims):
    def dot(a, b):
        return lax.dot_general(a, b, (dims, ((), ())), preferred_element_type=jnp.float32)

    return dot(left[0], right[0]) + (dot(left[0], right[1]) + dot(left[1], right[0]))


def slot_terms(left, right, pos, neg):
    left, right = split(left), split(right)
    sig = jax.nn.sigmoid(product(left, right, ((1,), (1,))))
    grad = split(neg * sig - pos * (1.0 - sig))
    return product(grad, right, ((1,), (0,))), product(grad, left, ((0,), (0,)))


def call(kernel, name, out_shape, in_specs, args, cost, scratch=()):
    several = isinstance(out_shape, tuple)
    return pl.pallas_call(
        kernel,
        out_shape=out_shape,
        in_specs=in_specs,
        out_specs=(IN_VMEM,) * len(out_shape) if several else IN_VMEM,
        scratch_shapes=scratch,
        compiler_params=PARAMS,
        cost_estimate=pl.CostEstimate(flops=int(cost * 1e9), bytes_accessed=0, transcendentals=0),
        name=name,
    )(*args)


def in_hbm(x):
    return pltpu.with_memory_space_constraint(x, pltpu.HBM)


def note_rows(values):
    row = lax.broadcasted_iota(jnp.int32, (NOTE_ROWS, TILE), 0)
    note = jnp.zeros((NOTE_ROWS, TILE), jnp.int32)
    for n, value in enumerate(values):
        note = jnp.where(row == n, value, note)
    return note.astype(jnp.float32)


def stage_pairs(meta, live, vert, ctx, pos, neg, row_tiles):
    def kernel(meta_ref, live_ref, vert_ref, ctx_ref, pos_ref, neg_ref, *refs):
        own_ref, vert_refs = refs[0], refs[1 : 1 + SUB]
        count_refs = refs[1 + SUB : -2]
        staged, sems = refs[-2:]
        odd = meta_ref[ODD_AT]
        copies = []
        for n, ref in enumerate((pos_ref, neg_ref)):
            copies.append(pltpu.make_async_copy(ref.at[0], staged.at[n], sems.at[n]))
        for s in range(SLOTS):
            rows = tile_rows(meta_ref[s * STEPS] % row_tiles)
            copies.append(pltpu.make_async_copy(ctx_ref.at[rows], own_ref.at[slot_rows(s)], sems.at[len(copies)]))
        for cls, out_ref in zip(CLASSES, vert_refs):
            for s in range(SLOTS):
                rows = tile_rows(meta_ref[s * STEPS + user_offset(cls, 0, odd)] // row_tiles)
                copies.append(pltpu.make_async_copy(vert_ref.at[rows], out_ref.at[slot_rows(s)], sems.at[len(copies)]))
        for copy in copies:
            copy.start()
        for copy in copies:
            copy.wait()
        for m, out_ref in enumerate(count_refs):
            k = user_offset(CLASSES[m % SUB], m // SUB, odd)
            for n in range(2):
                for s in range(SLOTS):
                    live = s < live_ref[0, k]
                    out_ref[slot_rows(s, n), :] = jnp.where(live, staged[n, k, s].astype(jnp.float32), 0.0)
            out_ref[2 * PAIR_ROWS :, :] = note_rows([meta_ref[s * STEPS + k] % row_tiles for s in range(SLOTS)])

    n_copies = 2 + SLOTS * (1 + SUB)
    own, *rest = call(
        kernel,
        "stage",
        (PAIR,) * (1 + SUB) + (COUNTS,) * (2 * SUB),
        [IN_SMEM] * 2 + [IN_HBM] * 4,
        [meta, live, in_hbm(vert), in_hbm(ctx), in_hbm(pos), in_hbm(neg)],
        2,
        [pltpu.VMEM((2, STEPS, SLOTS, TILE, TILE), jnp.int32), pltpu.SemaphoreType.DMA((n_copies,))],
    )
    keys = [(cls, epoch) for epoch in range(2) for cls in CLASSES]
    return own, dict(zip(CLASSES, rest)), dict(zip(keys, rest[SUB:]))


def select_columns(meta, ctx, cls, row_tiles):
    def kernel(meta_ref, ctx_ref, out_ref):
        k = user_offset(cls, 0, meta_ref[ODD_AT])
        for s in range(SLOTS):
            out_ref[slot_rows(s), :] = ctx_ref[tile_rows(meta_ref[s * STEPS + k] % row_tiles), :]

    return call(kernel, f"select_{cls}", PAIR, [IN_SMEM, IN_VMEM], [meta, ctx], 1)


def pair_terms(rows, cols, counts, noted, name):
    def kernel(rows_ref, cols_ref, counts_ref, gv_ref, gc_ref):
        for s in range(SLOTS):
            gv_ref[slot_rows(s), :], gc_ref[slot_rows(s), :] = slot_terms(
                rows_ref[slot_rows(s), :],
                cols_ref[slot_rows(s), :],
                counts_ref[slot_rows(s), :],
                counts_ref[slot_rows(s, 1), :],
            )
        if noted:
            gc_ref[PAIR_ROWS:, :] = counts_ref[2 * PAIR_ROWS :, :]

    return call(kernel, name, (PAIR, NOTED if noted else PAIR), [IN_VMEM] * 3, [rows, cols, counts], 4)


def apply_vertex(meta, vert, grads, epoch, row_tiles):
    def kernel(meta_ref, vert_ref, *refs):
        grad_refs, out_ref, next_refs = refs[:SUB], refs[SUB], refs[SUB + 1 :]
        odd = meta_ref[ODD_AT]
        out_ref[...] = vert_ref[...]
        for cls, grad_ref in zip(CLASSES, grad_refs):
            for s in range(SLOTS):
                rows = tile_rows(meta_ref[s * STEPS + user_offset(cls, epoch, odd)] // row_tiles)
                out_ref[rows, :] -= RATES[epoch] * grad_ref[slot_rows(s), :]
        for cls, next_ref in zip(CLASSES, next_refs):
            for s in range(SLOTS):
                rows = tile_rows(meta_ref[s * STEPS + user_offset(cls, 1, odd)] // row_tiles)
                next_ref[slot_rows(s), :] = out_ref[rows, :]

    shapes = (jax.ShapeDtypeStruct(vert.shape, vert.dtype),) + (PAIR,) * (SUB if epoch == 0 else 0)
    args = [meta, vert] + [grads[cls] for cls in CLASSES]
    return call(kernel, f"vertex_{epoch}", shapes, [IN_SMEM] + [IN_VMEM] * (1 + SUB), args, 1)


def first_context(meta, ctx, rows, cols, counts, row_tiles):
    def kernel(meta_ref, ctx_ref, rows_ref, cols_ref, counts_ref, gv_ref, out_ref):
        out_ref[...] = ctx_ref[...]
        for s in range(SLOTS):
            gv_ref[slot_rows(s), :], grad = slot_terms(
                rows_ref[slot_rows(s), :],
                cols_ref[slot_rows(s), :],
                counts_ref[slot_rows(s), :],
                counts_ref[slot_rows(s, 1), :],
            )
            out_ref[tile_rows(meta_ref[s * STEPS] % row_tiles), :] -= RATES[0] * grad

    shapes = (PAIR, jax.ShapeDtypeStruct(ctx.shape, ctx.dtype))
    args = [meta, ctx, rows, cols, counts]
    return call(kernel, "first_context", shapes, [IN_SMEM] + [IN_VMEM] * 4, args, 4)


def gather_context(near, ctx, grads, row_tiles):
    def kernel(near_ref, ctx_ref, *refs):
        grad_refs, out_ref, send_refs = refs[: SUB - 1], refs[SUB - 1], refs[SUB:]
        odd = near_ref[0, ODD_AT]
        tiles = []
        for grad_ref in grad_refs:
            for s in range(SLOTS):
                tiles.append(jnp.max(grad_ref[PAIR_ROWS + s : PAIR_ROWS + s + 1, :]).astype(jnp.int32))
        out_ref[...] = ctx_ref[...]
        for n, grad_ref in enumerate(grad_refs):
            for s in range(SLOTS):
                out_ref[tile_rows(tiles[n * SLOTS + s]), :] -= RATES[0] * grad_ref[slot_rows(s), :]
        for cls, send_ref in zip(CLASSES, send_refs):
            for s in range(SLOTS):
                tile = near_ref[cls, s * STEPS + owner_offset(cls, 1, odd)] % row_tiles
                send_ref[slot_rows(s), :] = out_ref[tile_rows(tile), :]

    shapes = (jax.ShapeDtypeStruct(ctx.shape, ctx.dtype),) + (PAIR,) * SUB
    return call(kernel, "gather_context", shapes, [IN_SMEM] + [IN_VMEM] * SUB, [near, ctx, *grads], 1)


def returned_context(near, ctx, rows, cols, counts, row_tiles):
    n_rows = ctx.shape[0]

    def kernel(near_ref, ctx_ref, rows_ref, cols_ref, counts_ref, gv_ref, out_ref):
        odd = near_ref[0, ODD_AT]
        out_ref[:n_rows, :] = ctx_ref[...]
        for s in range(SLOTS):
            gv_ref[slot_rows(s), :], grad = slot_terms(
                rows_ref[slot_rows(s), :],
                cols_ref[slot_rows(s), :],
                counts_ref[slot_rows(s), :],
                counts_ref[slot_rows(s, 1), :],
            )
            out_ref[tile_rows(near_ref[0, s * STEPS + SUB] % row_tiles), :] -= RATES[1] * grad
        notes = []
        for cls in OTHERS:
            for s in range(SLOTS):
                notes.append(near_ref[cls, s * STEPS + owner_offset(cls, 1, odd)] % row_tiles)
        out_ref[n_rows:, :] = note_rows(notes)

    shapes = (PAIR, jax.ShapeDtypeStruct((n_rows + NOTE_ROWS, TILE), ctx.dtype))
    args = [near, ctx, rows, cols, counts]
    return call(kernel, "returned_context", shapes, [IN_SMEM] + [IN_VMEM] * 4, args, 4)


def last_context(notes, ctx, grads):
    rows = ctx.shape[0] - NOTE_ROWS

    def kernel(notes_ref, ctx_ref, *refs):
        *grad_refs, out_ref = refs
        out_ref[...] = ctx_ref[:rows, :]
        for n, grad_ref in enumerate(grad_refs):
            for s in range(SLOTS):
                out_ref[tile_rows(notes_ref[n * SLOTS + s]), :] -= RATES[1] * grad_ref[slot_rows(s), :]

    shape = jax.ShapeDtypeStruct((rows, TILE), ctx.dtype)
    return call(kernel, "last_context", shape, [IN_SMEM] + [IN_VMEM] * SUB, [notes, ctx, *grads], 1)


def per_device(vertex, context, tile_ids, live_tiles, pos_counts, neg_counts):
    row_tiles = vertex.shape[0] // TILE
    odd = (lax.axis_index("blk") & 1)[None]
    pad = jnp.zeros((META - ODD_AT - 1,), jnp.int32)
    meta = jnp.concatenate([jnp.swapaxes(tile_ids, 1, 2).reshape(-1), odd, pad])

    ids = {0: meta}
    for cls in OTHERS:
        ids[cls] = to_owners(meta, cls)
    ids[3], ids[2], ids[1] = lax.optimization_barrier((ids[3], ids[2], ids[1]))
    own, rows, counts = stage_pairs(meta, live_tiles, vertex, context, pos_counts, neg_counts, row_tiles)
    cols = {cls: to_users(select_columns(ids[cls], context, cls, row_tiles), cls) for cls in OTHERS}
    gv, gc = {}, {}
    gv[0], handed = first_context(meta, context, rows[0], own, counts[0, 0], row_tiles)
    handed = to_users(handed, 0, SUB)
    for cls in OTHERS:
        gv[cls], gc[cls] = pair_terms(rows[cls], cols[cls], counts[cls, 0], True, f"terms_0_{cls}")
        gc[cls] = to_users(gc[cls], cls)
    near = jnp.stack([ids[cls] for cls in range(SUB)])
    vert, *rows = apply_vertex(meta, vertex, gv, 0, row_tiles)
    ctx, *cols = gather_context(near, handed, [gc[cls] for cls in OTHERS], row_tiles)

    rows, cols = dict(zip(CLASSES, rows)), dict(zip(CLASSES, cols))
    cols.update({cls: to_users(cols[cls], cls) for cls in OTHERS})
    gv[0], back = returned_context(near, ctx, rows[0], cols[0], counts[0, 1], row_tiles)
    back = to_owners(back, 0, SUB)
    notes = back[-NOTE_ROWS:, 0].astype(jnp.int32)
    for cls in OTHERS:
        gv[cls], grad = pair_terms(rows[cls], cols[cls], counts[cls, 1], False, f"terms_1_{cls}")
        gc[cls] = to_owners(grad, cls, SUB)
    (vert,) = apply_vertex(meta, vert, gv, 1, row_tiles)
    ctx = last_context(notes, back, [gc[cls] for cls in OTHERS])
    return vert, ctx


def solution(mesh):
    placed = (
        P(("ep", "blk"), None),
        P(("ep", "blk"), None),
        P(("ep", "blk"), None, None),
        P(("ep", "blk"), None),
        P(("ep", "blk"), None, None, None, None),
        P(("ep", "blk"), None, None, None, None),
    )
    return jax.shard_map(
        per_device,
        mesh=mesh,
        in_specs=placed,
        out_specs=(P(("ep", "blk"), None), P(("ep", "blk"), None)),
        check_vma=False,
    )
```

```python
import jax
import jax.numpy as jnp
from jax import lax
from jax.experimental import pallas as pl
from jax.experimental.pallas import tpu as pltpu
from jax.sharding import PartitionSpec as P

RATES = (0.02, 0.01)
TILE = 128
SLOTS = 2
SUB = 4
STEPS = 2 * SUB
CLASSES = (3, 2, 1, 0)
OTHERS = (3, 2, 1)
PAIR_ROWS = SLOTS * TILE
META = 32
ODD_AT = SLOTS * STEPS
NOTE_ROWS = 8
VMEM_BYTES = 8 * 1024 * 1024

IN_VMEM = pl.BlockSpec(memory_space=pltpu.VMEM)
IN_SMEM = pl.BlockSpec(memory_space=pltpu.SMEM)
IN_HBM = pl.BlockSpec(memory_space=pltpu.HBM)
PARAMS = pltpu.CompilerParams(vmem_limit_bytes=VMEM_BYTES)
PAIR = jax.ShapeDtypeStruct((PAIR_ROWS, TILE), jnp.float32)
NOTED = jax.ShapeDtypeStruct((PAIR_ROWS + NOTE_ROWS, TILE), jnp.float32)
COUNTS = jax.ShapeDtypeStruct((2 * PAIR_ROWS + NOTE_ROWS, TILE), jnp.float32)


def ahead(place, cls):
    return ((place ^ ((SUB - cls) % SUB)) - place) & (SUB - 1)


def to_users(block, cls, extra=0):
    size = lax.axis_size("blk")
    return lax.ppermute(block, "blk", [(j, (j + ahead(j % SUB, cls) + extra) % size) for j in range(size)])


def to_owners(block, cls, extra=0):
    size = lax.axis_size("blk")
    return lax.ppermute(block, "blk", [((j + ahead(j % SUB, cls) + extra) % size, j) for j in range(size)])


def user_offset(cls, epoch, odd):
    return SUB * epoch + (0, 1 + 2 * odd, 2, 3 - 2 * odd)[cls]


def owner_offset(cls, epoch, odd):
    return SUB * epoch + (0, 3 - 2 * odd, 2, 1 + 2 * odd)[cls]


def tile_rows(index):
    return pl.ds(pl.multiple_of(index * TILE, TILE), TILE)


def slot_rows(slot, part=0):
    return pl.ds(part * PAIR_ROWS + slot * TILE, TILE)


def split(x):
    high = x.astype(jnp.bfloat16)
    return high, (x - high.astype(jnp.float32)).astype(jnp.bfloat16)


def product(left, right, dims):
    def dot(a, b):
        return lax.dot_general(a, b, (dims, ((), ())), preferred_element_type=jnp.float32)

    return dot(left[0], right[0]) + (dot(left[0], right[1]) + dot(left[1], right[0]))


def slot_terms(left, right, pos, neg):
    left, right = split(left), split(right)
    sig = jax.nn.sigmoid(product(left, right, ((1,), (1,))))
    grad = split(neg * sig - pos * (1.0 - sig))
    return product(grad, right, ((1,), (0,))), product(grad, left, ((0,), (0,)))


def call(kernel, name, out_shape, in_specs, args, cost, scratch=()):
    several = isinstance(out_shape, tuple)
    return pl.pallas_call(
        kernel,
        out_shape=out_shape,
        in_specs=in_specs,
        out_specs=(IN_VMEM,) * len(out_shape) if several else IN_VMEM,
        scratch_shapes=scratch,
        compiler_params=PARAMS,
        cost_estimate=pl.CostEstimate(flops=int(cost * 1e9), bytes_accessed=0, transcendentals=0),
        name=name,
    )(*args)


def in_hbm(x):
    return pltpu.with_memory_space_constraint(x, pltpu.HBM)


def note_rows(values):
    row = lax.broadcasted_iota(jnp.int32, (NOTE_ROWS, TILE), 0)
    note = jnp.zeros((NOTE_ROWS, TILE), jnp.int32)
    for n, value in enumerate(values):
        note = jnp.where(row == n, value, note)
    return note.astype(jnp.float32)


def stage_pairs(meta, live, vert, ctx, pos, neg, row_tiles):
    def kernel(meta_ref, live_ref, vert_ref, ctx_ref, pos_ref, neg_ref, *refs):
        own_ref, vert_refs = refs[0], refs[1 : 1 + SUB]
        count_refs = refs[1 + SUB : -2]
        staged, sems = refs[-2:]
        odd = meta_ref[ODD_AT]
        copies = []
        for half in range(2):
            steps = pl.ds(SUB * half, SUB)
            for n, ref in enumerate((pos_ref, neg_ref)):
                copies.append(pltpu.make_async_copy(ref.at[0, steps], staged.at[n, steps], sems.at[len(copies)]))
        for s in range(SLOTS):
            rows = tile_rows(meta_ref[s * STEPS] % row_tiles)
            copies.append(pltpu.make_async_copy(ctx_ref.at[rows], own_ref.at[slot_rows(s)], sems.at[len(copies)]))
        for cls, out_ref in zip(CLASSES, vert_refs):
            for s in range(SLOTS):
                rows = tile_rows(meta_ref[s * STEPS + user_offset(cls, 0, odd)] // row_tiles)
                copies.append(pltpu.make_async_copy(vert_ref.at[rows], out_ref.at[slot_rows(s)], sems.at[len(copies)]))
        for copy in copies:
            copy.start()
        for m, out_ref in enumerate(count_refs):
            k = user_offset(CLASSES[m % SUB], m // SUB, odd)
            if m % SUB == 0:
                for copy in copies[2 * (m // SUB) : 2 * (m // SUB) + 2]:
                    copy.wait()
            for n in range(2):
                for s in range(SLOTS):
                    live = s < live_ref[0, k]
                    out_ref[slot_rows(s, n), :] = jnp.where(live, staged[n, k, s].astype(jnp.float32), 0.0)
            out_ref[2 * PAIR_ROWS :, :] = note_rows([meta_ref[s * STEPS + k] % row_tiles for s in range(SLOTS)])
        for copy in copies[4:]:
            copy.wait()

    n_copies = 4 + SLOTS * (1 + SUB)
    own, *rest = call(
        kernel,
        "stage",
        (PAIR,) * (1 + SUB) + (COUNTS,) * (2 * SUB),
        [IN_SMEM] * 2 + [IN_HBM] * 4,
        [meta, live, in_hbm(vert), in_hbm(ctx), in_hbm(pos), in_hbm(neg)],
        2,
        [pltpu.VMEM((2, STEPS, SLOTS, TILE, TILE), jnp.int32), pltpu.SemaphoreType.DMA((n_copies,))],
    )
    keys = [(cls, epoch) for epoch in range(2) for cls in CLASSES]
    return own, dict(zip(CLASSES, rest)), dict(zip(keys, rest[SUB:]))


def select_columns(meta, ctx, cls, row_tiles):
    def kernel(meta_ref, ctx_ref, out_ref):
        k = user_offset(cls, 0, meta_ref[ODD_AT])
        for s in range(SLOTS):
            out_ref[slot_rows(s), :] = ctx_ref[tile_rows(meta_ref[s * STEPS + k] % row_tiles), :]

    return call(kernel, f"select_{cls}", PAIR, [IN_SMEM, IN_VMEM], [meta, ctx], 1)


def pair_terms(rows, cols, counts, noted, name):
    def kernel(rows_ref, cols_ref, counts_ref, gv_ref, gc_ref):
        for s in range(SLOTS):
            gv_ref[slot_rows(s), :], gc_ref[slot_rows(s), :] = slot_terms(
                rows_ref[slot_rows(s), :],
                cols_ref[slot_rows(s), :],
                counts_ref[slot_rows(s), :],
                counts_ref[slot_rows(s, 1), :],
            )
        if noted:
            gc_ref[PAIR_ROWS:, :] = counts_ref[2 * PAIR_ROWS :, :]

    return call(kernel, name, (PAIR, NOTED if noted else PAIR), [IN_VMEM] * 3, [rows, cols, counts], 4)


def apply_vertex(meta, vert, grads, epoch, row_tiles):
    def kernel(meta_ref, vert_ref, *refs):
        grad_refs, out_ref, next_refs = refs[:SUB], refs[SUB], refs[SUB + 1 :]
        odd = meta_ref[ODD_AT]
        out_ref[...] = vert_ref[...]
        for cls, grad_ref in zip(CLASSES, grad_refs):
            for s in range(SLOTS):
                rows = tile_rows(meta_ref[s * STEPS + user_offset(cls, epoch, odd)] // row_tiles)
                out_ref[rows, :] -= RATES[epoch] * grad_ref[slot_rows(s), :]
        for cls, next_ref in zip(CLASSES, next_refs):
            for s in range(SLOTS):
                rows = tile_rows(meta_ref[s * STEPS + user_offset(cls, 1, odd)] // row_tiles)
                next_ref[slot_rows(s), :] = out_ref[rows, :]

    shapes = (jax.ShapeDtypeStruct(vert.shape, vert.dtype),) + (PAIR,) * (SUB if epoch == 0 else 0)
    args = [meta, vert] + [grads[cls] for cls in CLASSES]
    return call(kernel, f"vertex_{epoch}", shapes, [IN_SMEM] + [IN_VMEM] * (1 + SUB), args, 1)


def first_context(meta, ctx, rows, cols, counts, row_tiles):
    def kernel(meta_ref, ctx_ref, rows_ref, cols_ref, counts_ref, gv_ref, out_ref):
        out_ref[...] = ctx_ref[...]
        for s in range(SLOTS):
            gv_ref[slot_rows(s), :], grad = slot_terms(
                rows_ref[slot_rows(s), :],
                cols_ref[slot_rows(s), :],
                counts_ref[slot_rows(s), :],
                counts_ref[slot_rows(s, 1), :],
            )
            out_ref[tile_rows(meta_ref[s * STEPS] % row_tiles), :] -= RATES[0] * grad

    shapes = (PAIR, jax.ShapeDtypeStruct(ctx.shape, ctx.dtype))
    args = [meta, ctx, rows, cols, counts]
    return call(kernel, "first_context", shapes, [IN_SMEM] + [IN_VMEM] * 4, args, 4)


def gather_context(near, ctx, grads, row_tiles):
    def kernel(near_ref, ctx_ref, *refs):
        grad_refs, out_ref, send_refs = refs[: SUB - 1], refs[SUB - 1], refs[SUB:]
        odd = near_ref[0, ODD_AT]
        tiles = []
        for grad_ref in grad_refs:
            for s in range(SLOTS):
                tiles.append(jnp.max(grad_ref[PAIR_ROWS + s : PAIR_ROWS + s + 1, :]).astype(jnp.int32))
        out_ref[...] = ctx_ref[...]
        for n, grad_ref in enumerate(grad_refs):
            for s in range(SLOTS):
                out_ref[tile_rows(tiles[n * SLOTS + s]), :] -= RATES[0] * grad_ref[slot_rows(s), :]
        for cls, send_ref in zip(CLASSES, send_refs):
            for s in range(SLOTS):
                tile = near_ref[cls, s * STEPS + owner_offset(cls, 1, odd)] % row_tiles
                send_ref[slot_rows(s), :] = out_ref[tile_rows(tile), :]

    shapes = (jax.ShapeDtypeStruct(ctx.shape, ctx.dtype),) + (PAIR,) * SUB
    return call(kernel, "gather_context", shapes, [IN_SMEM] + [IN_VMEM] * SUB, [near, ctx, *grads], 1)


def returned_context(near, ctx, rows, cols, counts, row_tiles):
    n_rows = ctx.shape[0]

    def kernel(near_ref, ctx_ref, rows_ref, cols_ref, counts_ref, gv_ref, out_ref):
        odd = near_ref[0, ODD_AT]
        out_ref[:n_rows, :] = ctx_ref[...]
        for s in range(SLOTS):
            gv_ref[slot_rows(s), :], grad = slot_terms(
                rows_ref[slot_rows(s), :],
                cols_ref[slot_rows(s), :],
                counts_ref[slot_rows(s), :],
                counts_ref[slot_rows(s, 1), :],
            )
            out_ref[tile_rows(near_ref[0, s * STEPS + SUB] % row_tiles), :] -= RATES[1] * grad
        notes = []
        for cls in OTHERS:
            for s in range(SLOTS):
                notes.append(near_ref[cls, s * STEPS + owner_offset(cls, 1, odd)] % row_tiles)
        out_ref[n_rows:, :] = note_rows(notes)

    shapes = (PAIR, jax.ShapeDtypeStruct((n_rows + NOTE_ROWS, TILE), ctx.dtype))
    args = [near, ctx, rows, cols, counts]
    return call(kernel, "returned_context", shapes, [IN_SMEM] + [IN_VMEM] * 4, args, 4)


def last_context(notes, ctx, grads):
    rows = ctx.shape[0] - NOTE_ROWS

    def kernel(notes_ref, ctx_ref, *refs):
        *grad_refs, out_ref = refs
        out_ref[...] = ctx_ref[:rows, :]
        for n, grad_ref in enumerate(grad_refs):
            for s in range(SLOTS):
                out_ref[tile_rows(notes_ref[n * SLOTS + s]), :] -= RATES[1] * grad_ref[slot_rows(s), :]

    shape = jax.ShapeDtypeStruct((rows, TILE), ctx.dtype)
    return call(kernel, "last_context", shape, [IN_SMEM] + [IN_VMEM] * SUB, [notes, ctx, *grads], 1)


def per_device(vertex, context, tile_ids, live_tiles, pos_counts, neg_counts):
    row_tiles = vertex.shape[0] // TILE
    odd = (lax.axis_index("blk") & 1)[None]
    pad = jnp.zeros((META - ODD_AT - 1,), jnp.int32)
    meta = jnp.concatenate([jnp.swapaxes(tile_ids, 1, 2).reshape(-1), odd, pad])

    ids = {0: meta}
    for cls in OTHERS:
        ids[cls] = to_owners(meta, cls)
    ids[3], ids[2], ids[1] = lax.optimization_barrier((ids[3], ids[2], ids[1]))
    own, rows, counts = stage_pairs(meta, live_tiles, vertex, context, pos_counts, neg_counts, row_tiles)
    cols = {cls: to_users(select_columns(ids[cls], context, cls, row_tiles), cls) for cls in OTHERS}
    gv, gc = {}, {}
    gv[0], handed = first_context(meta, context, rows[0], own, counts[0, 0], row_tiles)
    handed = to_users(handed, 0, SUB)
    for cls in OTHERS:
        gv[cls], gc[cls] = pair_terms(rows[cls], cols[cls], counts[cls, 0], True, f"terms_0_{cls}")
        gc[cls] = to_users(gc[cls], cls)
    near = jnp.stack([ids[cls] for cls in range(SUB)])
    vert, *rows = apply_vertex(meta, vertex, gv, 0, row_tiles)
    ctx, *cols = gather_context(near, handed, [gc[cls] for cls in OTHERS], row_tiles)

    rows, cols = dict(zip(CLASSES, rows)), dict(zip(CLASSES, cols))
    cols.update({cls: to_users(cols[cls], cls) for cls in OTHERS})
    gv[0], back = returned_context(near, ctx, rows[0], cols[0], counts[0, 1], row_tiles)
    back = to_owners(back, 0, SUB)
    notes = back[-NOTE_ROWS:, 0].astype(jnp.int32)
    for cls in OTHERS:
        gv[cls], grad = pair_terms(rows[cls], cols[cls], counts[cls, 1], False, f"terms_1_{cls}")
        gc[cls] = to_owners(grad, cls, SUB)
    (vert,) = apply_vertex(meta, vert, gv, 1, row_tiles)
    ctx = last_context(notes, back, [gc[cls] for cls in OTHERS])
    return vert, ctx


def solution(mesh):
    placed = (
        P(("ep", "blk"), None),
        P(("ep", "blk"), None),
        P(("ep", "blk"), None, None),
        P(("ep", "blk"), None),
        P(("ep", "blk"), None, None, None, None),
        P(("ep", "blk"), None, None, None, None),
    )
    return jax.shard_map(
        per_device,
        mesh=mesh,
        in_specs=placed,
        out_specs=(P(("ep", "blk"), None), P(("ep", "blk"), None)),
        check_vma=False,
    )
```
